256 devices in a mesh: ctx: 32 (over z, x), head: 8 (over y, core).
Axes of the slice: x: 4, y: 4, z: 8, core: 2. Of those that a mesh axis runs over, the one named last changes fastest.
Arguments:
- lin_q: bfloat16 [12288, 4096], P('ctx', 'head'), may hold values from -6 to 6
- lin_k: bfloat16 [12288, 4096], P('ctx', 'head'), may hold values from -6 to 6
- lin_v: bfloat16 [12288, 4096], P('ctx', 'head'), may hold values from -16 to 16
- lin_decay: float32 [12288, 32], P('ctx', 'head'), may hold values from 0 to 1
- soft_q: bfloat16 [12288, 4096], P('ctx', 'head'), may hold values from -6 to 6
- soft_k: bfloat16 [12288, 1024], P('ctx', 'head'), may hold values from -6 to 6
- soft_v: bfloat16 [12288, 1024], P('ctx', 'head'), may hold values from -6 to 6
Outputs:
- lin_out: float32 [12288, 4096], P('ctx', 'head')
- soft_out: float32 [12288, 4096], P('ctx', 'head')
The draws below stay inside these ranges and needn't reach their ends.
All inputs are finite; a program needn't handle non-finite values.
Results may differ from the reference program's by a relative error of at most 0.004.
Values may be sent and summed in bfloat16 or wider, within the bound.
A program may use at most 64 MiB of HBM per device.

```python
import math
import jax
import jax.numpy as jnp
from jax import lax

HEAD_DIM = 128
HEADS_LIN = 32
HEADS_Q = 32
KV_HEADS = 8
ROWS_DEV = 384
ROLLOUT_LENGTH = 12288


def draw_lin_v(key, part):
    key = jax.random.fold_in(key, 12)
    columns = jnp.arange(HEADS_LIN * HEAD_DIM)
    head_frac = (columns // HEAD_DIM).astype(jnp.float32) / max(HEADS_LIN - 1, 1)
    base = jnp.clip(jax.random.normal(key, (ROLLOUT_LENGTH, HEADS_LIN * HEAD_DIM), jnp.float32), -4.0, 4.0)
    return (base * jnp.power(3.0, head_frac)[None, :]).astype(jnp.bfloat16)


def decay_law(key, fast_count):
    random_subkeys = jax.random.split(key, 7)
    order = jax.random.permutation(random_subkeys[0], HEADS_LIN)
    fast = order < fast_count
    fast_rate = jnp.exp(jax.random.uniform(random_subkeys[1], (HEADS_LIN,), jnp.float32, math.log(1.0 / 50.0), math.log(1.0 / 30.0)))
    slow_rate = jnp.exp(jax.random.uniform(random_subkeys[2], (HEADS_LIN,), jnp.float32, math.log(0.04), math.log(0.4))) / ROLLOUT_LENGTH
    decay_speed = jnp.where(fast, fast_rate, slow_rate)
    block_multiplier = jnp.exp(jax.random.uniform(random_subkeys[3], (ROLLOUT_LENGTH // ROWS_DEV, HEADS_LIN), jnp.float32, math.log(0.5), math.log(2.0)))
    block_multiplier = jnp.repeat(block_multiplier, ROWS_DEV, axis=0)
    approximate_result = jnp.exp(jax.random.uniform(random_subkeys[4], (ROLLOUT_LENGTH, HEADS_LIN), jnp.float32, math.log(0.6), math.log(1.8)))
    window_rows = jax.random.randint(random_subkeys[5], (2,), 0, ROLLOUT_LENGTH)
    window_length = -jnp.log(1.0 - jax.random.uniform(random_subkeys[6], (2,), jnp.float32, 0.2, 0.5))
    position_indices = jnp.arange(ROLLOUT_LENGTH)
    window_span = jnp.zeros((ROLLOUT_LENGTH,), jnp.float32)
    for item_count in range(2):
        window_span = window_span + jnp.where(position_indices == window_rows[item_count], window_length[item_count], 0.0)
    return decay_speed[None, :] * block_multiplier * approximate_result + window_span[:, None]


def draw_lin_decay(key, part):
    key = jax.random.fold_in(key, 11)
    return decay_law(key, HEADS_LIN // 2)


def draw_soft_q(key, part):
    key = jax.random.fold_in(key, 13)
    width = HEADS_Q * HEAD_DIM
    return jnp.clip(jax.random.normal(key, (ROLLOUT_LENGTH, width), jnp.float32), -4.0, 4.0).astype(jnp.bfloat16)


def draw_soft_k(key, part):
    key = jax.random.fold_in(key, 14)
    width = KV_HEADS * HEAD_DIM
    return jnp.clip(jax.random.normal(key, (ROLLOUT_LENGTH, width), jnp.float32), -4.0, 4.0).astype(jnp.bfloat16)


def block_scale(stream_key, shape, cuts, smallest, high):
    level, own = 1.0, jax.random.fold_in(stream_key, 6)
    for axis_at, parts in cuts:
        draws = jnp.exp(jax.random.uniform(jax.random.fold_in(own, axis_at), (parts,), jnp.float32, smallest / len(cuts), high / len(cuts)))
        level = level * jnp.repeat(draws, shape[axis_at] // parts).reshape([-1 if axis == axis_at else 1 for axis in range(len(shape))])
    return level


def bell_draw(rng, shape, scale, reach, pieces=(), kind=jnp.bfloat16):
    values = jax.random.normal(rng, shape, jnp.float32) * scale
    if len(pieces) > 0:
        values = block_scale(rng, shape, pieces, -0.22, 0.18) * values
    return jnp.clip(values, min=-reach, max=reach).astype(kind)


def setup_inputs(seed: int = 0) -> dict:
    keys = jax.random.split(jax.random.key(seed), 8)
    lin_q = bell_draw(keys[0], (ROLLOUT_LENGTH, HEADS_LIN * HEAD_DIM), 1.0, 6.0, ((0, 32), (1, 8)))
    lin_k = bell_draw(keys[1], (ROLLOUT_LENGTH, HEADS_LIN * HEAD_DIM), 1.0, 6.0, ((0, 32), (1, 8)))
    lin_v = draw_lin_v(jax.random.fold_in(keys[7], 71), 0)
    lin_decay = draw_lin_decay(jax.random.fold_in(keys[7], 71), 0)
    soft_q = draw_soft_q(jax.random.fold_in(keys[7], 71), 0)
    soft_k = draw_soft_k(jax.random.fold_in(keys[7], 71), 0)
    soft_v = bell_draw(keys[6], (ROLLOUT_LENGTH, KV_HEADS * HEAD_DIM), 1.0, 6.0, ((0, 32), (1, 8)))
    return dict(lin_q=lin_q, lin_k=lin_k, lin_v=lin_v, lin_decay=lin_decay, soft_q=soft_q, soft_k=soft_k, soft_v=soft_v)


NEG_LARGE = -1e+30

def lightning_block(block_q, block_k, block_v, block_decay):
    row_count = block_q.shape[0]
    q_heads = block_q.astype(jnp.float32).reshape(row_count, HEADS_LIN, HEAD_DIM)
    k_heads = block_k.astype(jnp.float32).reshape(row_count, HEADS_LIN, HEAD_DIM)
    v_heads = block_v.astype(jnp.float32).reshape(row_count, HEADS_LIN, HEAD_DIM)
    cumulative = jnp.cumsum(block_decay, axis=0)
    scores = jnp.einsum('thd,shd->hts', q_heads, k_heads, precision=lax.Precision.HIGHEST)
    position_indices = jnp.arange(row_count, dtype=jnp.int32)
    causal = position_indices[:, None] >= position_indices[None, :]
    column_cum = jnp.transpose(cumulative)
    spread = column_cum[:, :, None] - column_cum[:, None, :]
    weights = jnp.where(causal[None], scores * jnp.exp(-jnp.maximum(spread, 0.0)), 0.0)
    rounded = lax.optimization_barrier(weights.astype(jnp.bfloat16)).astype(jnp.float32)
    intra = jnp.einsum('hts,she->the', rounded, v_heads, precision=lax.Precision.HIGHEST)
    final_cum = cumulative[-1]
    decay_gain = jnp.exp(-final_cum)
    scaled_keys = k_heads * jnp.exp(cumulative - final_cum)[:, :, None]
    local_state = jnp.einsum('shd,she->hde', scaled_keys, v_heads, precision=lax.Precision.HIGHEST)
    return (q_heads, intra, decay_gain, local_state, cumulative)

def reference(lin_q, lin_k, lin_v, lin_decay, soft_q, soft_k, soft_v):
    block_count = ROLLOUT_LENGTH // ROWS_DEV

    def advance(chain_state, block_number):
        first = (block_number * ROWS_DEV).astype(jnp.int32)
        q_heads, intra, decay_gain, local_state, cumulative = lightning_block(lax.dynamic_slice_in_dim(lin_q, first, ROWS_DEV, 0), lax.dynamic_slice_in_dim(lin_k, first, ROWS_DEV, 0), lax.dynamic_slice_in_dim(lin_v, first, ROWS_DEV, 0), lax.dynamic_slice_in_dim(lin_decay, first, ROWS_DEV, 0))
        inter = jnp.einsum('thd,hde->the', q_heads, chain_state, precision=lax.Precision.HIGHEST)
        mixed = intra + jnp.exp(-cumulative)[:, :, None] * inter
        updated = decay_gain[:, None, None] * chain_state + local_state
        return (updated, mixed)
    start_state = jnp.zeros((HEADS_LIN, HEAD_DIM, HEAD_DIM), jnp.float32)
    _, mixed_all = lax.scan(advance, start_state, jnp.arange(block_count, dtype=jnp.int32))
    mixed_all = mixed_all.reshape(ROLLOUT_LENGTH, HEADS_LIN, HEAD_DIM)
    mean_square = lax.optimization_barrier(jnp.mean(mixed_all * mixed_all, axis=(1, 2)))
    lin_out = (mixed_all * lax.rsqrt(mean_square + 1e-05)[:, None, None]).reshape(ROLLOUT_LENGTH, HEADS_LIN * HEAD_DIM)
    group_size = HEADS_Q // KV_HEADS
    score_scale = 1.0 / math.sqrt(HEAD_DIM)
    keys_all = soft_k.astype(jnp.float32).reshape(ROLLOUT_LENGTH, KV_HEADS, HEAD_DIM)
    values_all = soft_v.astype(jnp.float32).reshape(ROLLOUT_LENGTH, KV_HEADS, HEAD_DIM)
    key_positions = jnp.arange(ROLLOUT_LENGTH, dtype=jnp.int32)

    def soft_block(block_number):
        first = (block_number * ROWS_DEV).astype(jnp.int32)
        queries = lax.dynamic_slice_in_dim(soft_q, first, ROWS_DEV, 0).astype(jnp.float32)
        queries = queries.reshape(ROWS_DEV, KV_HEADS, group_size, HEAD_DIM)
        query_positions = first + jnp.arange(ROWS_DEV, dtype=jnp.int32)
        visible = query_positions[:, None] >= key_positions[None, :]

        def per_head(head_number):
            head_queries = jnp.take(queries, head_number, axis=1)
            head_keys = jnp.take(keys_all, head_number, axis=1)
            head_values = jnp.take(values_all, head_number, axis=1)
            scores = jnp.einsum('rgd,sd->grs', head_queries, head_keys, precision=lax.Precision.HIGHEST) * score_scale
            scores = jnp.where(visible[None], scores, NEG_LARGE)
            largest = lax.optimization_barrier(jnp.max(scores, axis=-1, keepdims=True))
            exponents = jnp.where(visible[None], jnp.exp(scores - largest), 0.0)
            prob_total = lax.optimization_barrier(jnp.sum(exponents, axis=-1))
            rounded = lax.optimization_barrier(exponents.astype(jnp.bfloat16)).astype(jnp.float32)
            weighted = jnp.einsum('grs,sd->grd', rounded, head_values, precision=lax.Precision.HIGHEST)
            return weighted / prob_total[:, :, None]
        head_outputs = lax.map(per_head, jnp.arange(KV_HEADS, dtype=jnp.int32))
        return jnp.transpose(head_outputs, (2, 0, 1, 3)).reshape(ROWS_DEV, HEADS_Q * HEAD_DIM)
    soft_all = lax.map(soft_block, jnp.arange(block_count, dtype=jnp.int32))
    soft_out = soft_all.reshape(ROLLOUT_LENGTH, HEADS_Q * HEAD_DIM)
    return (lin_out, soft_out)
```

```python
import math

import jax
import jax.numpy as jnp
from jax import lax
from jax.experimental import pallas as pl
from jax.experimental.pallas import tpu as pltpu
from jax.sharding import PartitionSpec as P

MESH = pl.DeviceIdType.MESH
F32 = jnp.float32
BF16 = jnp.bfloat16
D = 128
R = 384
NX = 4
NZ = 8
NH = 4
MODEL = 4096
HIGHEST = lax.Precision.HIGHEST
SCALE = math.log2(math.e) / math.sqrt(D)
START = -1e30
HIDDEN = -2e30

A_BT = (((1,), (1,)), ((), ()))


def dot(a, b):
    return jnp.dot(a, b, preferred_element_type=F32)


def split(a):
    high = a.astype(BF16)
    return high, (a - high.astype(F32)).astype(BF16)


def kernel(
    lq, lk, lv, ld, sq, sk, sv, lin_out, soft_out,
    kb, vb, qb, acc, mx, ob, ls, orv, lrv,
    mixed, cums, p1s, p1r, p2r, p3s, p3r, ssr,
    k_rs, v_rs, k_ss, v_ss, q_rs, q_ss, o_rs, o_ss, l_rs, l_ss,
    p1_rs, p1_ss, p2_rs, p2_ss, p3_rs, p3_ss, s_rs, s_ss,
):
    c = lax.axis_index("ctx")
    hd = lax.axis_index("head")
    z = c // NX
    x = c % NX

    def at_z(dz):
        return (lax.rem(z + dz + NZ, NZ) * NX + x, hd)

    def at_x(dx):
        return (z * NX + lax.rem(x + dx + NX, NX), hd)

    def at_h(dh):
        return (c, lax.rem(hd + dh, 8))

    def rows(r):
        return pl.ds(pl.multiple_of(r * R, R), R)

    def row_of(dz):
        return lax.rem(z + dz + NZ, NZ)

    def remote(src, dst, ss, rs, dev):
        return pltpu.make_async_remote_copy(
            src_ref=src, dst_ref=dst, send_sem=ss, recv_sem=rs, device_id=dev, device_id_type=MESH
        )

    def k_copy(dz, way):
        r = row_of(dz)
        n = 0 if dz == 0 and way > 0 else (1 if dz == 0 else (1 + abs(dz) if way > 0 else 4 + abs(dz)))
        return remote(kb.at[rows(r), :], kb.at[rows(r), :], k_ss.at[n], k_rs.at[r], at_z(way))

    def v_copy(dz, way):
        r = row_of(dz)
        n = 0 if dz == 0 and way > 0 else (1 if dz == 0 else (1 + abs(dz) if way > 0 else 4 + abs(dz)))
        part = vb.at[pl.ds(0, D), rows(r)]
        return remote(part, part, v_ss.at[n], v_rs.at[r], at_z(way))

    k_sends = [(0, 1), (0, -1), (-1, 1), (1, -1), (-2, 1), (2, -1), (-3, 1)]
    v_sends = [(0, 1), (0, -1), (-1, 1), (1, -1), (-2, 1), (2, -1), (3, -1)]

    def tile_of(slot, h):
        return h if slot == 0 else (4 + 2 * h if slot == 1 else (5 + 2 * h if slot == 2 else 12 + h))

    def q_copy(slot, h):
        t = tile_of(slot, h)
        dx = {1: -1, 2: 1, 3: 2}[slot]
        return remote(
            sq.at[:, pl.ds(h * D, D)], qb.at[t], q_ss.at[t - 4], q_rs.at[t - 4], at_x(dx)
        )

    def o_copy(slot, h, count):
        dx = {1: 1, 2: -1, 3: 2}[slot]
        part = pl.ds(h, count)
        n = 2 * (slot - 1) + h // 2
        return remote(
            ob.at[slot - 1, part], orv.at[slot - 1, part], o_ss.at[n], o_rs.at[n], at_x(dx)
        )

    def l_copy(slot):
        dx = {1: 1, 2: -1, 3: 2}[slot]
        return remote(
            ls.at[slot - 1], lrv.at[slot - 1], l_ss.at[slot - 1], l_rs.at[slot - 1], at_x(dx)
        )

    def p1_copy(dx):
        there = lax.rem(x + dx, NX)
        return remote(p1s.at[there], p1r.at[x], p1_ss.at[dx], p1_rs.at[x], at_x(dx))

    def p1_wait(dx):
        there = lax.rem(x + dx, NX)
        remote(p1s.at[there], p1r.at[there], p1_ss.at[dx], p1_rs.at[there], at_x(dx)).wait_recv()

    def p2_copy(dz):
        return remote(p2r.at[z], p2r.at[z], p2_ss.at[dz], p2_rs.at[z], at_z(dz))

    def p2_wait(dz):
        r = z - dz
        remote(p2r.at[r], p2r.at[r], p2_ss.at[dz], p2_rs.at[r], at_z(dz)).wait_recv()

    def p3_copy(dx):
        there = lax.rem(x + dx, NX)
        return remote(p3s.at[there], p3r.at[x], p3_ss.at[dx], p3_rs.at[x], at_x(dx))

    def p3_wait(dx):
        there = lax.rem(x + dx, NX)
        remote(p3s.at[there], p3r.at[there], p3_ss.at[dx], p3_rs.at[there], at_x(dx)).wait_recv()

    def s_copy(dh):
        return remote(ssr.at[hd], ssr.at[hd], s_ss.at[dh], s_rs.at[hd], at_h(dh))

    def s_wait(dh):
        there = lax.rem(hd + dh, 8)
        remote(ssr.at[there], ssr.at[there], s_ss.at[dh], s_rs.at[there], at_h(dh)).wait_recv()

    barrier = pltpu.get_barrier_semaphore()
    for dz in range(1, NZ):
        pl.semaphore_signal(barrier, inc=1, device_id=at_z(dz), device_id_type=MESH)
    for dx in range(1, NX):
        pl.semaphore_signal(barrier, inc=1, device_id=at_x(dx), device_id_type=MESH)
    for dh in range(1, 8):
        pl.semaphore_signal(barrier, inc=1, device_id=at_h(dh), device_id_type=MESH)

    kb[rows(z), :] = sk[...]
    vb[pl.ds(0, D), rows(z)] = sv[...].T
    vb[pl.ds(D, 16), :] = jnp.ones((16, NZ * R), BF16)
    for h in range(NH):
        qb[h] = sq[:, h * D : (h + 1) * D]
    pl.semaphore_wait(barrier, 17)

    for way in (1, -1):
        k_copy(0, way).start()
        v_copy(0, way).start()
    for h in range(NH):
        q_copy(1, h).start()
        q_copy(2, h).start()
    for h in range(NH):
        q_copy(3, h).start()

    t_at = lax.broadcasted_iota(jnp.int32, (R, R), 0)
    s_at = lax.broadcasted_iota(jnp.int32, (R, R), 1)
    causal = t_at >= s_at
    cum = jnp.dot(causal.astype(F32), ld[...], precision=HIGHEST, preferred_element_type=F32)
    cum = jnp.concatenate([cum, jnp.zeros((R, D - NH), F32)], axis=1)
    cums[...] = cum
    cum_row = cum.T
    for h in range(NH):
        cols = slice(h * D, (h + 1) * D)
        qh, kh, vh = lq[:, cols], lk[:, cols], lv[:, cols]
        cum_t = cum[:, h : h + 1]
        cum_s = cum_row[h : h + 1, :]
        last = cum[R - 1 : R, h : h + 1]
        scores = lax.dot_general(qh, kh, A_BT, preferred_element_type=F32)
        weights = jnp.where(causal, scores * jnp.exp(-jnp.maximum(cum_t - cum_s, 0.0)), 0.0)
        mixed[:, cols] = dot(weights.astype(BF16), vh)
        scaled = kh.astype(F32) * jnp.exp(cum_t - last)
        high, low = split(scaled)
        p1s[h, 0:D, :] = dot(high.T, vh) + dot(low.T, vh)
        p1s[h, D : D + 8, :] = jnp.broadcast_to(last, (8, D))
    for dx in range(1, NX):
        p1_copy(dx).start()
    p1r[x] = p1s[x]

    for_all = jnp.full((8, R), START, F32)
    for t in range(16):
        mx[t] = for_all
        acc[t] = jnp.zeros((D + 16, R), F32)

    diff = s_at - t_at

    def block(i, base, size, masked):
        sub = 768 if size == 768 else 512
        parts = size // sub

        def score(j):
            q = qb[4 * i + j]
            out = []
            for n in range(parts):
                keys = kb[pl.ds(pl.multiple_of(base + n * sub, R if sub == 768 else D), sub), :]
                out.append(lax.dot_general(keys, q, A_BT, preferred_element_type=F32))
            return out

        def finish(j, ps, al):
            total = acc[4 * i + j] * al
            for n in range(parts):
                values = vb[:, pl.ds(pl.multiple_of(base + n * sub, D), sub)]
                total = total + dot(values, ps[n])
            acc[4 * i + j] = total

        now = score(0)
        pending = None
        for j in range(4):
            later = score(j + 1) if j < 3 else None
            if pending is not None:
                finish(*pending)
            if masked:
                dx = jnp.where(i == 0, 0, jnp.where(i == 3, 2, 1 if j % 2 == 0 else -1))
                there = lax.rem(x + dx + NX, NX)
                first = base // R
                halves = []
                for half in range(2):
                    lead = (NX * (z - first - half) + there - x) * R
                    seen = diff + lead >= 0
                    halves.append(jnp.where(seen, now[0][half * R : (half + 1) * R], HIDDEN))
                now = halves
            top = now[0].max(axis=0, keepdims=True)
            for n in range(1, len(now)):
                top = jnp.maximum(top, now[n].max(axis=0, keepdims=True))
            old = mx[4 * i + j, 0:1, :]
            new = jnp.maximum(old, top * SCALE)
            al = jnp.exp2(old - new)
            mx[4 * i + j, 0:1, :] = new
            ps = [jnp.exp2(s * SCALE - new).astype(BF16) for s in now]
            if masked:
                ps = [jnp.concatenate(ps, axis=0)]
            pending = (j, ps, al)
            now = later
        finish(*pending)

    def closed(t):
        l = jnp.maximum(acc[t, D : D + 1, :], 1e-35)
        return acc[t, 0:D, :] / l, mx[t, 0:1, :] + jnp.log2(l)

    def close(slot, heads):
        for h in heads:
            o, lse = closed(tile_of(slot, h))
            ob[slot - 1, h] = o.astype(BF16)
            ls[slot - 1, h : h + 1, :] = lse

    def lin_totals():
        for dx in range(1, NX):
            p1_wait(dx)
        total = p1r[0, 0:D, :]
        lead = p1r[0, D : D + 8, :]
        for n in range(1, NX):
            g = p1r[n, D : D + 8, :]
            total = total * jnp.exp(-g[0:1]) + p1r[n, 0:D, :]
            lead = lead + g
        p2r[z, 0:D, :] = total
        p2r[z, D : D + 8, :] = lead
        for dz in range(1, NZ):
            @pl.when(z + dz < NZ)
            def _():
                p2_copy(dz).start()

    def lin_prefix():
        p3s[0] = jnp.zeros((D, D), F32)
        for dz in range(NZ - 1, 0, -1):
            @pl.when(z - dz >= 0)
            def _():
                p2_wait(dz)
                r = z - dz
                g = p2r[r, D : D + 8, :]
                p3s[0] = p3s[0] * jnp.exp(-g[0:1]) + p2r[r, 0:D, :]

        for n in range(1, NX):
            g = p1r[n - 1, D : D + 8, :]
            p3s[n] = p3s[n - 1] * jnp.exp(-g[0:1]) + p1r[n - 1, 0:D, :]
        for dx in range(1, NX):
            p3_copy(dx).start()
        p3r[x] = p3s[x]

    def lin_mix():
        for dx in range(1, NX):
            p3_wait(dx)
        square = jnp.zeros((R, D), F32)
        for h in range(NH):
            cols = slice(h * D, (h + 1) * D)
            high, low = split(p3r[h])
            qh = lq[:, cols]
            inter = dot(qh, high) + dot(qh, low)
            m = mixed[:, cols] + jnp.exp(-cums[:, h : h + 1]) * inter
            mixed[:, cols] = m
            square = square + m * m
        ssr[hd] = lax.dot_general(
            jnp.ones((8, D), F32), square, A_BT, precision=HIGHEST, preferred_element_type=F32
        )
        for dh in range(1, 8):
            s_copy(dh).start()

    def z_step(d):
        if d < 4:
            wait_k(-d)
            wait_v(-d)
            wait_k(d)
            wait_v(d)
        else:
            wait_k(4)
            wait_v(4)
        for dz, way in k_sends:
            if abs(dz) == d:
                k_copy(dz, way).start()
        for dz, way in v_sends:
            if abs(dz) == d:
                v_copy(dz, way).start()

    def wait_k(dz):
        r = row_of(dz)
        part = kb.at[rows(r), :]
        remote(part, part, k_ss.at[0], k_rs.at[r], at_z(1)).wait_recv()

    def wait_v(dz):
        r = row_of(dz)
        part = vb.at[pl.ds(0, D), rows(r)]
        remote(part, part, v_ss.at[0], v_rs.at[r], at_z(1)).wait_recv()

    own = 2 * (z // 2) * R

    def step(n, carry):
        is_a = (n <= 2) | (n == 6)
        is_b = ((n >= 3) & (n <= 5)) | (n == 7)
        i = jnp.where(
            n <= 2, n, jnp.where(n <= 5, n - 3, jnp.where(n <= 8, 3, jnp.where(n == 11, 0, n - 8)))
        )

        @pl.when(n == 0)
        def _():
            z_step(1)

        @pl.when(n == 1)
        def _():
            for h in (0, 1):
                q_copy(1, h).wait_recv()
                q_copy(2, h).wait_recv()

        @pl.when(n == 2)
        def _():
            z_step(2)
            lin_totals()
            for h in (2, 3):
                q_copy(1, h).wait_recv()
                q_copy(2, h).wait_recv()

        @pl.when(n == 5)
        def _():
            z_step(3)
            lin_prefix()

        @pl.when(n == 6)
        def _():
            for h in range(NH):
                q_copy(3, h).wait_recv()

        @pl.when(n == 8)
        def _():
            z_step(4)
            lin_mix()

        @pl.when(is_a)
        def _():
            block(i, own, 768, True)

        @pl.when(is_b & ((z == 7) | ((z % 2 == 0) & (z > 0))))
        def _():
            block(i, jnp.where(z == 7, 0, (z - 2) * R), 768, False)

        @pl.when((n >= 8) & (z >= 5))
        def _():
            block(i, jnp.where(z == 7, 2 * R, 0), 1536, False)

        @pl.when((n >= 8) & ((z == 3) | (z == 4)))
        def _():
            block(i, 0 * z, 768, False)

        @pl.when(n == 8)
        def _():
            close(3, range(NH))
            l_copy(3).start()
            o_copy(3, 0, 2).start()
            o_copy(3, 2, 2).start()

        @pl.when(n == 9)
        def _():
            for slot in (1, 2):
                close(slot, (0, 1))
                o_copy(slot, 0, 2).start()

        @pl.when(n == 10)
        def _():
            for slot in (1, 2):
                close(slot, (2, 3))
                o_copy(slot, 2, 2).start()
                l_copy(slot).start()

        return carry

    lax.fori_loop(0, 12, step, 0)

    for dh in range(1, 8):
        s_wait(dh)
    square = ssr[0]
    for n in range(1, 8):
        square = square + ssr[n]
    scale = lax.rsqrt(square[0:1, :] * (1.0 / MODEL) + 1e-05)
    scale = jnp.broadcast_to(scale, (D, R)).T
    for h in range(NH):
        cols = slice(h * D, (h + 1) * D)
        lin_out[:, cols] = mixed[:, cols] * scale

    for slot in (3, 1, 2):
        l_copy(slot).wait_recv()
    for h in range(NH):
        if h % 2 == 0:
            for slot in (3, 1, 2):
                o_copy(slot, h, 2).wait_recv()
        o, lse = closed(h)
        others = [lrv[n, h : h + 1, :] for n in range(3)]
        top = lse
        for one in others:
            top = jnp.maximum(top, one)
        w = jnp.exp2(lse - top)
        total = w
        o = o * w
        for n in range(3):
            w = jnp.exp2(others[n] - top)
            total = total + w
            o = o + orv[n, h].astype(F32) * w
        soft_out[:, h * D : (h + 1) * D] = (o / total).T

    for dz, way in k_sends:
        k_copy(dz, way).wait_send()
    for dz, way in v_sends:
        v_copy(dz, way).wait_send()
    for slot in (1, 2, 3):
        for h in range(NH):
            q_copy(slot, h).wait_send()
        for h in (0, 2):
            o_copy(slot, h, 2).wait_send()
        l_copy(slot).wait_send()
    for dx in range(1, NX):
        p1_copy(dx).wait_send()
        p3_copy(dx).wait_send()
    for dz in range(1, NZ):
        @pl.when(z + dz < NZ)
        def _():
            p2_copy(dz).wait_send()
    for dh in range(1, 8):
        s_copy(dh).wait_send()


def body(lin_q, lin_k, lin_v, lin_decay, soft_q, soft_k, soft_v):
    dma = pltpu.SemaphoreType.DMA
    vmem = pl.BlockSpec(memory_space=pltpu.VMEM)
    out = jax.ShapeDtypeStruct((R, NH * D), F32)
    return pl.pallas_call(
        kernel,
        out_shape=(out, out),
        in_specs=[vmem] * 7,
        out_specs=(vmem, vmem),
        scratch_shapes=[
            pltpu.VMEM((NZ * R, D), BF16),
            pltpu.VMEM((D + 16, NZ * R), BF16),
            pltpu.VMEM((16, R, D), BF16),
            pltpu.VMEM((16, D + 16, R), F32),
            pltpu.VMEM((16, 8, R), F32),
            pltpu.VMEM((3, NH, D, R), BF16),
            pltpu.VMEM((3, 8, R), F32),
            pltpu.VMEM((3, NH, D, R), BF16),
            pltpu.VMEM((3, 8, R), F32),
            pltpu.VMEM((R, NH * D), F32),
            pltpu.VMEM((R, D), F32),
            pltpu.VMEM((NX, D + 8, D), F32),
            pltpu.VMEM((NX, D + 8, D), F32),
            pltpu.VMEM((NZ, D + 8, D), F32),
            pltpu.VMEM((NX, D, D), F32),
            pltpu.VMEM((NX, D, D), F32),
            pltpu.VMEM((8, 8, R), F32),
            dma((8,)), dma((8,)), dma((8,)), dma((8,)),
            dma((12,)), dma((12,)), dma((6,)), dma((6,)), dma((3,)), dma((3,)),
            dma((4,)), dma((4,)), dma((8,)), dma((8,)), dma((4,)), dma((4,)), dma((8,)), dma((8,)),
        ],
        compiler_params=pltpu.CompilerParams(
            collective_id=0, has_side_effects=True, vmem_limit_bytes=48 << 20
        ),
    )(lin_q, lin_k, lin_v, lin_decay, soft_q, soft_k, soft_v)


def solution(mesh):
    spec = P("ctx", "head")
    return jax.shard_map(
        body, mesh=mesh, in_specs=(spec,) * 7, out_specs=(spec, spec), check_vma=False
    )
```

```python
import math

import jax
import jax.numpy as jnp
from jax import lax
from jax.experimental import pallas as pl
from jax.experimental.pallas import tpu as pltpu
from jax.sharding import PartitionSpec as P

MESH = pl.DeviceIdType.MESH
F32 = jnp.float32
BF16 = jnp.bfloat16
D = 128
R = 384
NX = 4
NZ = 8
NH = 4
MODEL = 4096
HIGHEST = lax.Precision.HIGHEST
SCALE = math.log2(math.e) / math.sqrt(D)
START = -1e30
HIDDEN = -2e30

A_BT = (((1,), (1,)), ((), ()))


def dot(a, b):
    return jnp.dot(a, b, preferred_element_type=F32)


def three(a):
    high = a.astype(BF16)
    rest = a - high.astype(F32)
    middle = rest.astype(BF16)
    low = (rest - middle.astype(F32)).astype(BF16)
    at = lax.broadcasted_iota(jnp.int32, (16, D), 0)
    rows = [jnp.broadcast_to(p[0:1].astype(F32), (16, D)) for p in (high, middle, low)]
    out = jnp.where(at == 0, rows[0], jnp.where(at == 1, rows[1], jnp.where(at == 2, rows[2], 0.0)))
    return out.astype(BF16)


def whole(part):
    part = part.astype(F32)
    return part[0:1] + part[1:2] + part[2:3]


def split(a):
    high = a.astype(BF16)
    return high, (a - high.astype(F32)).astype(BF16)


def kernel(
    lq_in, lk_in, lv_in, ld_in, sq, sk_in, sv_in, lin_out, soft_out,
    lq, lk, lv, ld, sv, in_sem, kb, vb, qb, acc, mx, ob, ls, orv, lrv,
    mixed, cums, p1s, p1r, tot, before, p2s, p2r, p3s, p3r, ssr,
    k_rs, v_rs, k_ss, v_ss, q_rs, q_ss, o_rs, o_ss, l_rs, l_ss,
    p1_rs, p1_ss, p2_rs, p2_ss, p3_rs, p3_ss, s_rs, s_ss,
):
    c = lax.axis_index("ctx")
    hd = lax.axis_index("head")
    z = c // NX
    x = c % NX

    def at_z(dz):
        return (lax.rem(z + dz + NZ, NZ) * NX + x, hd)

    def at_x(dx):
        return (z * NX + lax.rem(x + dx + NX, NX), hd)

    def at_h(dh):
        return (c, lax.rem(hd + dh, 8))

    def rows(r):
        return pl.ds(pl.multiple_of(r * R, R), R)

    def row_of(dz):
        return lax.rem(z + dz + NZ, NZ)

    def remote(src, dst, ss, rs, dev):
        return pltpu.make_async_remote_copy(
            src_ref=src, dst_ref=dst, send_sem=ss, recv_sem=rs, device_id=dev, device_id_type=MESH
        )

    def k_copy(dz, way):
        r = row_of(dz)
        n = 0 if dz == 0 and way > 0 else (1 if dz == 0 else (1 + abs(dz) if way > 0 else 4 + abs(dz)))
        return remote(kb.at[rows(r), :], kb.at[rows(r), :], k_ss.at[n], k_rs.at[r], at_z(way))

    def v_copy(dz, way):
        r = row_of(dz)
        n = 0 if dz == 0 and way > 0 else (1 if dz == 0 else (1 + abs(dz) if way > 0 else 4 + abs(dz)))
        part = vb.at[pl.ds(0, D), rows(r)]
        return remote(part, part, v_ss.at[n], v_rs.at[r], at_z(way))

    k_sends = [(0, 1), (0, -1), (-1, 1), (1, -1), (-2, 1), (2, -1), (-3, 1)]
    v_sends = [(0, 1), (0, -1), (-1, 1), (1, -1), (-2, 1), (2, -1), (3, -1)]

    def tile_of(slot, h):
        return (h, 4 + 2 * ((h + 2) % 4), 5 + 2 * h, 12 + h)[slot]

    def q_copy(slot, h):
        t = tile_of(slot, h)
        if slot < 3:
            src, dx = sq.at[:, pl.ds(h * D, D)], (-1 if slot == 1 else 1)
        elif h < 2:
            src, dx = qb.at[tile_of(2, h)], 1
        else:
            src, dx = qb.at[tile_of(1, h)], -1
        return remote(src, qb.at[t], q_ss.at[t - 4], q_rs.at[t - 4], at_x(dx))

    def o_copy(slot, h):
        dx = (1 if h == 0 else -1) if slot == 3 else (1 if slot == 1 else -1)
        part = pl.ds(h, 2)
        n = 2 * (slot - 1) + h // 2
        return remote(
            ob.at[slot - 1, part], orv.at[slot - 1, part], o_ss.at[n], o_rs.at[n], at_x(dx)
        )

    def l_copy(n):
        dx = (1, -1, 1, -1)[n]
        return remote(ls.at[min(n, 2)], lrv.at[n], l_ss.at[n], l_rs.at[n], at_x(dx))

    def p1_copy(dx):
        there = lax.rem(x + dx, NX)
        return remote(p1s.at[there], p1r.at[x], p1_ss.at[dx], p1_rs.at[x], at_x(dx))

    def p1_wait(dx):
        there = lax.rem(x + dx, NX)
        remote(p1s.at[there], p1r.at[there], p1_ss.at[dx], p1_rs.at[there], at_x(dx)).wait_recv()

    def p2_copy(n, dz):
        return remote(p2s.at[n], p2r.at[n], p2_ss.at[n, dz], p2_rs.at[n], at_z(dz))

    def p2_sends(n):
        return (z % 2 == 0, z % 4 == 1, z == 3)[n]

    def p3_copy(dx):
        there = lax.rem(x + dx, NX)
        return remote(p3s.at[there], p3r.at[x], p3_ss.at[dx], p3_rs.at[x], at_x(dx))

    def p3_wait(dx):
        there = lax.rem(x + dx, NX)
        remote(p3s.at[there], p3r.at[there], p3_ss.at[dx], p3_rs.at[there], at_x(dx)).wait_recv()

    def s_copy(dh):
        return remote(ssr.at[hd], ssr.at[hd], s_ss.at[dh], s_rs.at[hd], at_h(dh))

    def s_wait(dh):
        there = lax.rem(hd + dh, 8)
        remote(ssr.at[there], ssr.at[there], s_ss.at[dh], s_rs.at[there], at_h(dh)).wait_recv()

    places = [(sk_in, kb.at[rows(z), :]), (sv_in, sv), (ld_in, ld), (lk_in, lk), (lv_in, lv), (lq_in, lq)]
    places += [(sq.at[:, pl.ds(h * D, D)], qb.at[h]) for h in range(NH)]
    loads = [pltpu.make_async_copy(a, b, in_sem.at[n]) for n, (a, b) in enumerate(places)]
    for load in loads:
        load.start()
    barrier = pltpu.get_barrier_semaphore()
    for dz in range(1, NZ):
        pl.semaphore_signal(barrier, inc=1, device_id=at_z(dz), device_id_type=MESH)
    for dx in range(1, NX):
        pl.semaphore_signal(barrier, inc=1, device_id=at_x(dx), device_id_type=MESH)
    for dh in range(1, 8):
        pl.semaphore_signal(barrier, inc=1, device_id=at_h(dh), device_id_type=MESH)

    vb[pl.ds(D, 16), :] = jnp.ones((16, NZ * R), BF16)
    loads[1].wait()
    vb[pl.ds(0, D), rows(z)] = sv[...].T
    loads[0].wait()
    pl.semaphore_wait(barrier, 17)

    for way in (1, -1):
        k_copy(0, way).start()
        v_copy(0, way).start()
    q_copy(1, 2).start()
    q_copy(2, 0).start()

    t_at = lax.broadcasted_iota(jnp.int32, (R, R), 0)
    s_at = lax.broadcasted_iota(jnp.int32, (R, R), 1)
    causal = t_at >= s_at
    loads[2].wait()
    decay = jnp.concatenate([ld[...], jnp.zeros((D - NH, R), F32)], axis=0)
    cum_row = lax.dot_general(
        decay, causal.astype(F32), A_BT, precision=HIGHEST, preferred_element_type=F32
    )
    cum = cum_row.T
    cums[...] = cum
    for n in (3, 4):
        loads[n].wait()
    for h in range(NH):
        cols = slice(h * D, (h + 1) * D)
        kh, vh = lk[:, cols], lv[:, cols]
        last = cum[R - 1 : R, h : h + 1]
        high, low = split(kh.astype(F32) * jnp.exp(cum[:, h : h + 1] - last))
        p1s[h, 0:D, :] = (dot(high.T, vh) + dot(low.T, vh)).astype(BF16)
        p1s[h, D : D + 16, :] = three(jnp.broadcast_to(last, (8, D)))
    for dx in range(1, NX):
        p1_copy(dx).start()
    p1r[x] = p1s[x]
    q_copy(1, 3).start()
    q_copy(2, 1).start()
    for h in (0, 1):
        q_copy(1, h).start()
        q_copy(2, h + 2).start()
    loads[5].wait()
    for h in range(NH):
        cols = slice(h * D, (h + 1) * D)
        qh, kh, vh = lq[:, cols], lk[:, cols], lv[:, cols]
        spread = cum[:, h : h + 1] - cum_row[h : h + 1, :]
        scores = lax.dot_general(qh, kh, A_BT, preferred_element_type=F32)
        weights = jnp.where(causal, scores * jnp.exp(-jnp.maximum(spread, 0.0)), 0.0)
        mixed[:, cols] = dot(weights.astype(BF16), vh)

    for_all = jnp.full((8, R), START, F32)
    for t in range(16):
        mx[t] = for_all
        acc[t] = jnp.zeros((D + 16, R), F32)

    diff = s_at - t_at

    def block(i, base, size, masked):
        sub = 768 if size == 768 else 512
        parts = size // sub

        def score(j):
            q = qb[4 * i + j]
            out = []
            for n in range(parts):
                keys = kb[pl.ds(pl.multiple_of(base + n * sub, R if sub == 768 else D), sub), :]
                out.append(lax.dot_general(keys, q, A_BT, preferred_element_type=F32))
            return out

        def finish(j, ps, al):
            total = acc[4 * i + j] * al
            for n in range(parts):
                values = vb[:, pl.ds(pl.multiple_of(base + n * sub, D), sub)]
                total = total + dot(values, ps[n])
            acc[4 * i + j] = total

        now = score(0)
        pending = None
        for j in range(4):
            later = score(j + 1) if j < 3 else None
            if pending is not None:
                finish(*pending)
            if masked:
                dx = jnp.where(i == 0, 0, jnp.where(i == 3, 2, 1 if j % 2 == 0 else -1))
                there = lax.rem(x + dx + NX, NX)
                first = base // R
                halves = []
                for half in range(2):
                    lead = (NX * (z - first - half) + there - x) * R
                    seen = diff + lead >= 0
                    halves.append(jnp.where(seen, now[0][half * R : (half + 1) * R], HIDDEN))
                now = halves
            top = now[0].max(axis=0, keepdims=True)
            for n in range(1, len(now)):
                top = jnp.maximum(top, now[n].max(axis=0, keepdims=True))
            old = mx[4 * i + j, 0:1, :]
            new = jnp.maximum(old, top * SCALE)
            al = jnp.exp2(old - new)
            mx[4 * i + j, 0:1, :] = new
            ps = [jnp.exp2(s * SCALE - new).astype(BF16) for s in now]
            if masked:
                ps = [jnp.concatenate(ps, axis=0)]
            pending = (j, ps, al)
            now = later
        finish(*pending)

    def closed(t):
        l = jnp.maximum(acc[t, D : D + 1, :], 1e-35)
        return acc[t, 0:D, :] / l, mx[t, 0:1, :] + jnp.log2(l)

    def close(slot, heads, part=None):
        for h in heads:
            o, lse = closed(tile_of(slot, h))
            if part is not None:
                other = lrv[part, h : h + 1, :]
                top = jnp.maximum(lse, other)
                w, v = jnp.exp2(lse - top), jnp.exp2(other - top)
                o = (o * w + orv[2, h].astype(F32) * v) / (w + v)
                lse = top + jnp.log2(w + v)
            ob[slot - 1, h] = o.astype(BF16)
            ls[slot - 1, h : h + 1, :] = lse

    def lin_totals():
        for dx in range(1, NX):
            p1_wait(dx)
        total = p1r[0, 0:D, :].astype(F32)
        lead = whole(p1r[0, D : D + 16, :])
        for n in range(1, NX):
            g = whole(p1r[n, D : D + 16, :])
            total = total * jnp.exp(-g) + p1r[n, 0:D, :].astype(F32)
            lead = lead + g
        tot[0:D, :] = total
        tot[D : D + 8, :] = jnp.broadcast_to(lead, (8, D))
        before[...] = jnp.zeros((D + 8, D), F32)
        lin_send(0)

    def lin_send(n):
        @pl.when(p2_sends(n))
        def _():
            g = tot[D : D + 8, :]
            p2s[n, 0:D, :] = before[0:D, :] * jnp.exp(-g[0:1]) + tot[0:D, :]
            p2s[n, D : D + 8, :] = before[D : D + 8, :] + g
            for dz in range(1, 2**n + 1):
                p2_copy(n, dz).start()

    def lin_get(n):
        @pl.when((z % 2 == 1, z % 4 >= 2, z >= 4)[n])
        def _():
            p2_copy(n, 1).wait_recv()
            lead = before[D : D + 8, :]
            before[0:D, :] = p2r[n, 0:D, :] * jnp.exp(-lead[0:1]) + before[0:D, :]
            before[D : D + 8, :] = lead + p2r[n, D : D + 8, :]

    def lin_prefix():
        lin_get(2)
        state = before[0:D, :]
        p3s[0] = state.astype(BF16)
        for n in range(1, NX):
            g = whole(p1r[n - 1, D : D + 16, :])
            state = state * jnp.exp(-g) + p1r[n - 1, 0:D, :].astype(F32)
            p3s[n] = state.astype(BF16)
        for dx in range(1, NX):
            p3_copy(dx).start()
        p3r[x] = p3s[x]

    def lin_mix():
        for dx in range(1, NX):
            p3_wait(dx)
        square = jnp.zeros((R, D), F32)
        for h in range(NH):
            cols = slice(h * D, (h + 1) * D)
            inter = dot(lq[:, cols], p3r[h])
            m = mixed[:, cols] + jnp.exp(-cums[:, h : h + 1]) * inter
            mixed[:, cols] = m
            square = square + m * m
        ssr[hd] = lax.dot_general(
            jnp.ones((8, D), F32), square, A_BT, precision=HIGHEST, preferred_element_type=F32
        )
        for dh in range(1, 8):
            s_copy(dh).start()

    def z_step(d):
        for wait, copy, sends in ((wait_k, k_copy, k_sends), (wait_v, v_copy, v_sends)):
            for dz in (-d, d) if d < 4 else (4,):
                wait(dz)
                for there, way in sends:
                    if there == dz:
                        copy(dz, way).start()

    def wait_k(dz):
        r = row_of(dz)
        part = kb.at[rows(r), :]
        remote(part, part, k_ss.at[0], k_rs.at[r], at_z(1)).wait_recv()

    def wait_v(dz):
        r = row_of(dz)
        part = vb.at[pl.ds(0, D), rows(r)]
        remote(part, part, v_ss.at[0], v_rs.at[r], at_z(1)).wait_recv()

    own = 2 * (z // 2) * R

    def step(n, carry):
        is_a = (n <= 1) | (n == 3) | (n == 5)
        is_b = (n == 2) | (n == 4) | (n == 6) | (n == 10)
        is_c = ((n >= 7) & (n <= 9)) | (n == 11)
        i = jnp.where((n == 0) | (n >= 10), 0, jnp.where((n == 1) | (n == 2) | (n == 8), 1, 3))
        i = jnp.where((n == 3) | (n == 4) | (n == 9), 2, i)

        @pl.when(n == 0)
        def _():
            z_step(1)
            for load in loads[6:]:
                load.wait()

        @pl.when(n == 1)
        def _():
            for h in (0, 1):
                q_copy(2, h).wait_recv()
                q_copy(3, h).start()
                q_copy(1, h + 2).wait_recv()
                q_copy(3, h + 2).start()

        @pl.when(n == 2)
        def _():
            z_step(2)

        @pl.when(n == 3)
        def _():
            for h in (0, 1):
                q_copy(1, h).wait_recv()
                q_copy(2, h + 2).wait_recv()
            lin_totals()

        @pl.when(n == 4)
        def _():
            lin_get(0)
            lin_send(1)

        @pl.when(n == 5)
        def _():
            z_step(3)
            for h in range(NH):
                q_copy(3, h).wait_recv()

        @pl.when(n == 6)
        def _():
            lin_get(1)
            lin_send(2)

        @pl.when(n == 7)
        def _():
            z_step(4)

        @pl.when(n == 8)
        def _():
            lin_prefix()

        @pl.when(n == 10)
        def _():
            lin_mix()

        @pl.when(is_a)
        def _():
            block(i, own, 768, True)

        @pl.when(is_b & ((z == 7) | ((z % 2 == 0) & (z > 0))))
        def _():
            block(i, jnp.where(z == 7, 0, (z - 2) * R), 768, False)

        @pl.when(is_c & (z >= 5))
        def _():
            block(i, jnp.where(z == 7, 2 * R, 0), 1536, False)

        @pl.when(is_c & ((z == 3) | (z == 4)))
        def _():
            block(i, 0 * z, 768, False)

        @pl.when(n == 7)
        def _():
            close(3, range(NH))
            for m in (2, 3):
                l_copy(m).start()
            for h in (0, 2):
                o_copy(3, h).start()

        @pl.when(n == 8)
        def _():
            for slot, h in ((1, 2), (2, 0)):
                close(slot, (h, h + 1))
                o_copy(slot, h).start()

        @pl.when(n == 9)
        def _():
            for m, slot, h in ((2, 1, 0), (3, 2, 2)):
                l_copy(m).wait_recv()
                o_copy(3, h).wait_recv()
                close(slot, (h, h + 1), m)
                l_copy(slot - 1).start()
                o_copy(slot, h).start()

        return carry

    lax.fori_loop(0, 12, step, 0)

    for dh in range(1, 8):
        s_wait(dh)
    square = ssr[0]
    for n in range(1, 8):
        square = square + ssr[n]
    scale = lax.rsqrt(square[0:1, :] * (1.0 / MODEL) + 1e-05)
    scale = jnp.broadcast_to(scale, (D, R)).T
    for h in range(NH):
        cols = slice(h * D, (h + 1) * D)
        lin_out[:, cols] = mixed[:, cols] * scale

    for m in (0, 1):
        l_copy(m).wait_recv()
    for slot, h in ((1, 2), (2, 0), (1, 0), (2, 2)):
        o_copy(slot, h).wait_recv()
    for h in range(NH):
        o, lse = closed(h)
        others = [lrv[n, h : h + 1, :] for n in range(2)]
        top = jnp.maximum(lse, jnp.maximum(*others))
        w = jnp.exp2(lse - top)
        total = w
        o = o * w
        for n in range(2):
            w = jnp.exp2(others[n] - top)
            total = total + w
            o = o + orv[n, h].astype(F32) * w
        soft_out[:, h * D : (h + 1) * D] = (o / total).T

    for dz, way in k_sends:
        k_copy(dz, way).wait_send()
    for dz, way in v_sends:
        v_copy(dz, way).wait_send()
    for slot in (1, 2, 3):
        for h in range(NH):
            q_copy(slot, h).wait_send()
        for h in (0, 2):
            o_copy(slot, h).wait_send()
    for m in range(4):
        l_copy(m).wait_send()
    for dx in range(1, NX):
        p1_copy(dx).wait_send()
        p3_copy(dx).wait_send()
    for n in range(3):
        @pl.when(p2_sends(n))
        def _():
            for dz in range(1, 2**n + 1):
                p2_copy(n, dz).wait_send()
    for dh in range(1, 8):
        s_copy(dh).wait_send()


def body(lin_q, lin_k, lin_v, lin_decay, soft_q, soft_k, soft_v):
    dma = pltpu.SemaphoreType.DMA
    vmem = pl.BlockSpec(memory_space=pltpu.VMEM)
    out = jax.ShapeDtypeStruct((R, NH * D), F32)
    return pl.pallas_call(
        kernel,
        out_shape=(out, out),
        in_specs=[pl.BlockSpec(memory_space=pl.ANY)] * 7,
        out_specs=(vmem, vmem),
        scratch_shapes=[
            pltpu.VMEM((R, NH * D), BF16),
            pltpu.VMEM((R, NH * D), BF16),
            pltpu.VMEM((R, NH * D), BF16),
            pltpu.VMEM((NH, R), F32),
            pltpu.VMEM((R, D), BF16),
            dma((10,)),
            pltpu.VMEM((NZ * R, D), BF16),
            pltpu.VMEM((D + 16, NZ * R), BF16),
            pltpu.VMEM((16, R, D), BF16),
            pltpu.VMEM((16, D + 16, R), F32),
            pltpu.VMEM((16, 8, R), F32),
            pltpu.VMEM((3, NH, D, R), BF16),
            pltpu.VMEM((3, 8, R), F32),
            pltpu.VMEM((3, NH, D, R), BF16),
            pltpu.VMEM((4, 8, R), F32),
            pltpu.VMEM((R, NH * D), F32),
            pltpu.VMEM((R, D), F32),
            pltpu.VMEM((NX, D + 16, D), BF16),
            pltpu.VMEM((NX, D + 16, D), BF16),
            pltpu.VMEM((D + 8, D), F32),
            pltpu.VMEM((D + 8, D), F32),
            pltpu.VMEM((3, D + 8, D), F32),
            pltpu.VMEM((3, D + 8, D), F32),
            pltpu.VMEM((NX, D, D), BF16),
            pltpu.VMEM((NX, D, D), BF16),
            pltpu.VMEM((8, 8, R), F32),
            dma((8,)), dma((8,)), dma((8,)), dma((8,)),
            dma((12,)), dma((12,)), dma((6,)), dma((6,)), dma((4,)), dma((4,)),
            dma((4,)), dma((4,)), dma((3,)), dma((3, 5)), dma((4,)), dma((4,)), dma((8,)), dma((8,)),
        ],
        compiler_params=pltpu.CompilerParams(
            collective_id=0, has_side_effects=True, vmem_limit_bytes=56 << 20
        ),
    )(lin_q, lin_k, lin_v, lin_decay.T, soft_q, soft_k, soft_v)


def solution(mesh):
    spec = P("ctx", "head")
    return jax.shard_map(
        body, mesh=mesh, in_specs=(spec,) * 7, out_specs=(spec, spec), check_vma=False
    )
```

```python
import math

import jax
import jax.numpy as jnp
from jax import lax
from jax.experimental import pallas as pl
from jax.experimental.pallas import tpu as pltpu
from jax.sharding import PartitionSpec as P

MESH = pl.DeviceIdType.MESH
F32 = jnp.float32
BF16 = jnp.bfloat16
D = 128
R = 384
NX = 4
NZ = 8
NH = 4
MODEL = 4096
HIGHEST = lax.Precision.HIGHEST
SCALE = math.log2(math.e) / math.sqrt(D)
START = -1e30
HIDDEN = -2e30

A_BT = (((1,), (1,)), ((), ()))


def dot(a, b):
    return jnp.dot(a, b, preferred_element_type=F32)


def three(a):
    high = a.astype(BF16)
    rest = a - high.astype(F32)
    middle = rest.astype(BF16)
    low = (rest - middle.astype(F32)).astype(BF16)
    at = lax.broadcasted_iota(jnp.int32, (16, D), 0)
    rows = [jnp.broadcast_to(p[0:1].astype(F32), (16, D)) for p in (high, middle, low)]
    out = jnp.where(at == 0, rows[0], jnp.where(at == 1, rows[1], jnp.where(at == 2, rows[2], 0.0)))
    return out.astype(BF16)


def whole(part):
    part = part.astype(F32)
    return part[0:1] + part[1:2] + part[2:3]


def split(a):
    high = a.astype(BF16)
    return high, (a - high.astype(F32)).astype(BF16)


def kernel(
    lq_in, lk_in, lv_in, ld_in, sq, sk_in, sv_in, lin_out, soft_out,
    lq, lk, lv, ld, sv, in_sem, so, out_sem, kb, vb, qb, acc, mx, ob, ls, orv, lrv,
    mixed, cums, p1s, p1r, tot, before, p2s, p2r, p3s, p3r, ssr,
    k_rs, v_rs, k_ss, v_ss, q_rs, q_ss, o_rs, o_ss, l_rs, l_ss,
    p1_rs, p1_ss, p2_rs, p2_ss, p3_rs, p3_ss, s_rs, s_ss,
):
    c = lax.axis_index("ctx")
    hd = lax.axis_index("head")
    z = c // NX
    x = c % NX

    def at_z(dz):
        return (lax.rem(z + dz + NZ, NZ) * NX + x, hd)

    def at_x(dx):
        return (z * NX + lax.rem(x + dx + NX, NX), hd)

    def at_h(dh):
        return (c, lax.rem(hd + dh, 8))

    def rows(r):
        return pl.ds(pl.multiple_of(r * R, R), R)

    def row_of(dz):
        return lax.rem(z + dz + NZ, NZ)

    def remote(src, dst, ss, rs, dev):
        return pltpu.make_async_remote_copy(
            src_ref=src, dst_ref=dst, send_sem=ss, recv_sem=rs, device_id=dev, device_id_type=MESH
        )

    def k_copy(dz, way):
        r = row_of(dz)
        n = 0 if dz == 0 and way > 0 else (1 if dz == 0 else (1 + abs(dz) if way > 0 else 4 + abs(dz)))
        return remote(kb.at[rows(r), :], kb.at[rows(r), :], k_ss.at[n], k_rs.at[r], at_z(way))

    def v_copy(dz, way):
        r = row_of(dz)
        n = 0 if dz == 0 and way > 0 else (1 if dz == 0 else (1 + abs(dz) if way > 0 else 4 + abs(dz)))
        part = vb.at[pl.ds(0, D), rows(r)]
        return remote(part, part, v_ss.at[n], v_rs.at[r], at_z(way))

    k_sends = [(0, 1), (0, -1), (-1, 1), (1, -1), (-2, 1), (2, -1), (-3, 1)]
    v_sends = [(0, 1), (0, -1), (-1, 1), (1, -1), (-2, 1), (2, -1), (3, -1)]

    def tile_of(slot, h):
        return (h, 4 + 2 * ((h + 2) % 4), 5 + 2 * h, 12 + h)[slot]

    def q_copy(slot, h):
        t = tile_of(slot, h)
        if slot < 3:
            src, dx = sq.at[:, pl.ds(h * D, D)], (-1 if slot == 1 else 1)
        elif h < 2:
            src, dx = qb.at[tile_of(2, h)], 1
        else:
            src, dx = qb.at[tile_of(1, h)], -1
        return remote(src, qb.at[t], q_ss.at[t - 4], q_rs.at[t - 4], at_x(dx))

    def o_copy(slot, h):
        dx = (1 if h == 0 else -1) if slot == 3 else (1 if slot == 1 else -1)
        part = pl.ds(h, 2)
        n = 2 * (slot - 1) + h // 2
        return remote(
            ob.at[slot - 1, part], orv.at[slot - 1, part], o_ss.at[n], o_rs.at[n], at_x(dx)
        )

    def l_copy(n):
        dx = (1, -1, 1, -1)[n]
        return remote(ls.at[min(n, 2)], lrv.at[n], l_ss.at[n], l_rs.at[n], at_x(dx))

    def p1_copy(dx):
        there = lax.rem(x + dx, NX)
        return remote(p1s.at[there], p1r.at[x], p1_ss.at[dx], p1_rs.at[x], at_x(dx))

    def p1_wait(dx):
        there = lax.rem(x + dx, NX)
        remote(p1s.at[there], p1r.at[there], p1_ss.at[dx], p1_rs.at[there], at_x(dx)).wait_recv()

    def p2_copy(n, dz):
        return remote(p2s.at[n], p2r.at[n], p2_ss.at[n, dz], p2_rs.at[n], at_z(dz))

    def p2_sends(n):
        return (z % 2 == 0, z % 4 == 1, z == 3)[n]

    def p3_copy(dx):
        there = lax.rem(x + dx, NX)
        return remote(p3s.at[there], p3r.at[x], p3_ss.at[dx], p3_rs.at[x], at_x(dx))

    def p3_wait(dx):
        there = lax.rem(x + dx, NX)
        remote(p3s.at[there], p3r.at[there], p3_ss.at[dx], p3_rs.at[there], at_x(dx)).wait_recv()

    def s_copy(dh):
        return remote(ssr.at[hd], ssr.at[hd], s_ss.at[dh], s_rs.at[hd], at_h(dh))

    def s_wait(dh):
        there = lax.rem(hd + dh, 8)
        remote(ssr.at[there], ssr.at[there], s_ss.at[dh], s_rs.at[there], at_h(dh)).wait_recv()

    places = [(sk_in, kb.at[rows(z), :]), (sv_in, sv), (ld_in, ld), (lk_in, lk), (lv_in, lv), (lq_in, lq)]
    places += [(sq.at[:, pl.ds(h * D, D)], qb.at[h]) for h in range(NH)]
    loads = [pltpu.make_async_copy(a, b, in_sem.at[n]) for n, (a, b) in enumerate(places)]
    for load in loads:
        load.start()
    barrier = pltpu.get_barrier_semaphore()
    for dz in range(1, NZ):
        pl.semaphore_signal(barrier, inc=1, device_id=at_z(dz), device_id_type=MESH)
    for dx in range(1, NX):
        pl.semaphore_signal(barrier, inc=1, device_id=at_x(dx), device_id_type=MESH)
    for dh in range(1, 8):
        pl.semaphore_signal(barrier, inc=1, device_id=at_h(dh), device_id_type=MESH)

    vb[pl.ds(D, 16), :] = jnp.ones((16, NZ * R), BF16)
    loads[1].wait()
    vb[pl.ds(0, D), rows(z)] = sv[...].T
    loads[0].wait()
    pl.semaphore_wait(barrier, 17)

    for way in (1, -1):
        k_copy(0, way).start()
        v_copy(0, way).start()
    q_copy(1, 2).start()
    q_copy(2, 0).start()

    t_at = lax.broadcasted_iota(jnp.int32, (R, R), 0)
    s_at = lax.broadcasted_iota(jnp.int32, (R, R), 1)
    causal = t_at >= s_at
    loads[2].wait()
    decay = jnp.concatenate([ld[...], jnp.zeros((D - NH, R), F32)], axis=0)
    cum_row = lax.dot_general(
        decay, causal.astype(F32), A_BT, precision=HIGHEST, preferred_element_type=F32
    )
    cum = cum_row.T
    cums[...] = cum
    for n in (3, 4):
        loads[n].wait()
    for h in range(NH):
        cols = slice(h * D, (h + 1) * D)
        kh, vh = lk[:, cols], lv[:, cols]
        last = cum[R - 1 : R, h : h + 1]
        high, low = split(kh.astype(F32) * jnp.exp(cum[:, h : h + 1] - last))
        p1s[h, 0:D, :] = (dot(high.T, vh) + dot(low.T, vh)).astype(BF16)
        p1s[h, D : D + 16, :] = three(jnp.broadcast_to(last, (8, D)))
    for dx in range(1, NX):
        p1_copy(dx).start()
    p1r[x] = p1s[x]
    q_copy(1, 3).start()
    q_copy(2, 1).start()
    for h in (0, 1):
        q_copy(1, h).start()
        q_copy(2, h + 2).start()
    loads[5].wait()
    for h in range(NH):
        cols = slice(h * D, (h + 1) * D)
        qh, kh, vh = lq[:, cols], lk[:, cols], lv[:, cols]
        spread = cum[:, h : h + 1] - cum_row[h : h + 1, :]
        scores = lax.dot_general(qh, kh, A_BT, preferred_element_type=F32)
        weights = jnp.where(causal, scores * jnp.exp(-jnp.maximum(spread, 0.0)), 0.0)
        mixed[:, cols] = dot(weights.astype(BF16), vh)

    for_all = jnp.full((8, R), START, F32)
    for t in range(16):
        mx[t] = for_all
        acc[t] = jnp.zeros((D + 16, R), F32)

    diff = s_at - t_at

    def block(i, base, size, masked):
        sub = 768 if size == 768 else 512
        parts = size // sub

        def score(j):
            q = qb[4 * i + j]
            out = []
            for n in range(parts):
                keys = kb[pl.ds(pl.multiple_of(base + n * sub, R if sub == 768 else D), sub), :]
                out.append(lax.dot_general(keys, q, A_BT, preferred_element_type=F32))
            return out

        def finish(j, ps, al):
            total = acc[4 * i + j] * al
            for n in range(parts):
                values = vb[:, pl.ds(pl.multiple_of(base + n * sub, D), sub)]
                total = total + dot(values, ps[n])
            acc[4 * i + j] = total

        now = score(0)
        pending = None
        for j in range(4):
            later = score(j + 1) if j < 3 else None
            if pending is not None:
                finish(*pending)
            if masked:
                dx = jnp.where(i == 0, 0, jnp.where(i == 3, 2, 1 if j % 2 == 0 else -1))
                there = lax.rem(x + dx + NX, NX)
                first = base // R
                halves = []
                for half in range(2):
                    lead = (NX * (z - first - half) + there - x) * R
                    seen = diff + lead >= 0
                    halves.append(jnp.where(seen, now[0][half * R : (half + 1) * R], HIDDEN))
                now = halves
            top = now[0].max(axis=0, keepdims=True)
            for n in range(1, len(now)):
                top = jnp.maximum(top, now[n].max(axis=0, keepdims=True))
            old = mx[4 * i + j, 0:1, :]
            new = jnp.maximum(old, top * SCALE)
            al = jnp.exp2(old - new)
            mx[4 * i + j, 0:1, :] = new
            ps = [jnp.exp2(s * SCALE - new).astype(BF16) for s in now]
            if masked:
                ps = [jnp.concatenate(ps, axis=0)]
            pending = (j, ps, al)
            now = later
        finish(*pending)

    def closed(t):
        l = jnp.maximum(acc[t, D : D + 1, :], 1e-35)
        return acc[t, 0:D, :] / l, mx[t, 0:1, :] + jnp.log2(l)

    def close(slot, heads, part=None):
        for h in heads:
            o, lse = closed(tile_of(slot, h))
            if part is not None:
                other = lrv[part, h : h + 1, :]
                top = jnp.maximum(lse, other)
                w, v = jnp.exp2(lse - top), jnp.exp2(other - top)
                o = (o * w + orv[2, h].astype(F32) * v) / (w + v)
                lse = top + jnp.log2(w + v)
            ob[slot - 1, h] = o.astype(BF16)
            ls[slot - 1, h : h + 1, :] = lse

    def lin_totals():
        for dx in range(1, NX):
            p1_wait(dx)
        total = p1r[0, 0:D, :].astype(F32)
        lead = whole(p1r[0, D : D + 16, :])
        for n in range(1, NX):
            g = whole(p1r[n, D : D + 16, :])
            total = total * jnp.exp(-g) + p1r[n, 0:D, :].astype(F32)
            lead = lead + g
        tot[0:D, :] = total
        tot[D : D + 8, :] = jnp.broadcast_to(lead, (8, D))
        before[...] = jnp.zeros((D + 8, D), F32)
        lin_send(0)

    def lin_send(n):
        @pl.when(p2_sends(n))
        def _():
            g = tot[D : D + 8, :]
            p2s[n, 0:D, :] = before[0:D, :] * jnp.exp(-g[0:1]) + tot[0:D, :]
            p2s[n, D : D + 8, :] = before[D : D + 8, :] + g
            for dz in range(1, 2**n + 1):
                p2_copy(n, dz).start()

    def lin_get(n):
        @pl.when((z % 2 == 1, z % 4 >= 2, z >= 4)[n])
        def _():
            p2_copy(n, 1).wait_recv()
            lead = before[D : D + 8, :]
            before[0:D, :] = p2r[n, 0:D, :] * jnp.exp(-lead[0:1]) + before[0:D, :]
            before[D : D + 8, :] = lead + p2r[n, D : D + 8, :]

    def lin_prefix():
        lin_get(2)
        state = before[0:D, :]
        p3s[0] = state.astype(BF16)
        for n in range(1, NX):
            g = whole(p1r[n - 1, D : D + 16, :])
            state = state * jnp.exp(-g) + p1r[n - 1, 0:D, :].astype(F32)
            p3s[n] = state.astype(BF16)
        for dx in range(1, NX):
            p3_copy(dx).start()
        p3r[x] = p3s[x]

    def lin_mix():
        for dx in range(1, NX):
            p3_wait(dx)
        square = jnp.zeros((R, D), F32)
        for h in range(NH):
            cols = slice(h * D, (h + 1) * D)
            inter = dot(lq[:, cols], p3r[h])
            m = mixed[:, cols] + jnp.exp(-cums[:, h : h + 1]) * inter
            mixed[:, cols] = m
            square = square + m * m
        ssr[hd] = lax.dot_general(
            jnp.ones((8, D), F32), square, A_BT, precision=HIGHEST, preferred_element_type=F32
        )
        for dh in range(1, 8):
            s_copy(dh).start()

    def z_step(d):
        for wait, copy, sends in ((wait_k, k_copy, k_sends), (wait_v, v_copy, v_sends)):
            for dz in (-d, d) if d < 4 else (4,):
                wait(dz)
                for there, way in sends:
                    if there == dz:
                        copy(dz, way).start()

    def wait_k(dz):
        r = row_of(dz)
        part = kb.at[rows(r), :]
        remote(part, part, k_ss.at[0], k_rs.at[r], at_z(1)).wait_recv()

    def wait_v(dz):
        r = row_of(dz)
        part = vb.at[pl.ds(0, D), rows(r)]
        remote(part, part, v_ss.at[0], v_rs.at[r], at_z(1)).wait_recv()

    own = 2 * (z // 2) * R

    def step(n, carry):
        is_a = (n <= 1) | (n == 3) | (n == 5)
        is_b = (n == 2) | (n == 4) | (n == 6) | (n == 10)
        is_c = ((n >= 7) & (n <= 9)) | (n == 11)
        i = jnp.where((n == 0) | (n >= 10), 0, jnp.where((n == 1) | (n == 2) | (n == 8), 1, 3))
        i = jnp.where((n == 3) | (n == 4) | (n == 9), 2, i)

        @pl.when(n == 0)
        def _():
            z_step(1)
            for load in loads[6:]:
                load.wait()

        @pl.when(n == 1)
        def _():
            for h in (0, 1):
                q_copy(2, h).wait_recv()
                q_copy(3, h).start()
                q_copy(1, h + 2).wait_recv()
                q_copy(3, h + 2).start()

        @pl.when(n == 2)
        def _():
            z_step(2)

        @pl.when(n == 3)
        def _():
            for h in (0, 1):
                q_copy(1, h).wait_recv()
                q_copy(2, h + 2).wait_recv()
            lin_totals()

        @pl.when(n == 4)
        def _():
            lin_get(0)
            lin_send(1)

        @pl.when(n == 5)
        def _():
            z_step(3)
            for h in range(NH):
                q_copy(3, h).wait_recv()

        @pl.when(n == 6)
        def _():
            lin_get(1)
            lin_send(2)

        @pl.when(n == 7)
        def _():
            z_step(4)

        @pl.when(n == 8)
        def _():
            lin_prefix()

        @pl.when(n == 10)
        def _():
            lin_mix()

        @pl.when(is_a)
        def _():
            block(i, own, 768, True)

        @pl.when(is_b & ((z == 7) | ((z % 2 == 0) & (z > 0))))
        def _():
            block(i, jnp.where(z == 7, 0, (z - 2) * R), 768, False)

        @pl.when(is_c & (z >= 5))
        def _():
            block(i, jnp.where(z == 7, 2 * R, 0), 1536, False)

        @pl.when(is_c & ((z == 3) | (z == 4)))
        def _():
            block(i, 0 * z, 768, False)

        @pl.when(n == 7)
        def _():
            close(3, range(NH))
            for m in (2, 3):
                l_copy(m).start()
            for h in (0, 2):
                o_copy(3, h).start()

        @pl.when(n == 8)
        def _():
            for slot, h in ((1, 2), (2, 0)):
                close(slot, (h, h + 1))
                o_copy(slot, h).start()

        @pl.when(n == 9)
        def _():
            for m, slot, h in ((2, 1, 0), (3, 2, 2)):
                l_copy(m).wait_recv()
                o_copy(3, h).wait_recv()
                close(slot, (h, h + 1), m)
                l_copy(slot - 1).start()
                o_copy(slot, h).start()

        return carry

    lax.fori_loop(0, 12, step, 0)

    for dh in range(1, 8):
        s_wait(dh)
    square = ssr[0]
    for n in range(1, 8):
        square = square + ssr[n]
    scale = lax.rsqrt(square[0:1, :] * (1.0 / MODEL) + 1e-05)
    scale = jnp.broadcast_to(scale, (D, R)).T
    for h in range(NH):
        cols = slice(h * D, (h + 1) * D)
        mixed[:, cols] = mixed[:, cols] * scale
    stores = [pltpu.make_async_copy(mixed, lin_out, out_sem.at[NH])]
    stores[0].start()

    for m in (0, 1):
        l_copy(m).wait_recv()
    for slot, h in ((1, 2), (2, 0), (1, 0), (2, 2)):
        o_copy(slot, h).wait_recv()
    for h in range(NH):
        o, lse = closed(h)
        others = [lrv[n, h : h + 1, :] for n in range(2)]
        top = jnp.maximum(lse, jnp.maximum(*others))
        w = jnp.exp2(lse - top)
        total = w
        o = o * w
        for n in range(2):
            w = jnp.exp2(others[n] - top)
            total = total + w
            o = o + orv[n, h].astype(F32) * w
        cols = pl.ds(h * D, D)
        so[h] = (o / total).T
        stores.append(pltpu.make_async_copy(so.at[h], soft_out.at[:, cols], out_sem.at[h]))
        stores[-1].start()

    for dz, way in k_sends:
        k_copy(dz, way).wait_send()
    for dz, way in v_sends:
        v_copy(dz, way).wait_send()
    for slot in (1, 2, 3):
        for h in range(NH):
            q_copy(slot, h).wait_send()
        for h in (0, 2):
            o_copy(slot, h).wait_send()
    for m in range(4):
        l_copy(m).wait_send()
    for dx in range(1, NX):
        p1_copy(dx).wait_send()
        p3_copy(dx).wait_send()
    for n in range(3):
        @pl.when(p2_sends(n))
        def _():
            for dz in range(1, 2**n + 1):
                p2_copy(n, dz).wait_send()
    for dh in range(1, 8):
        s_copy(dh).wait_send()

    for store in stores:
        store.wait()

def body(lin_q, lin_k, lin_v, lin_decay, soft_q, soft_k, soft_v):
    dma = pltpu.SemaphoreType.DMA
    out = jax.ShapeDtypeStruct((R, NH * D), F32)
    return pl.pallas_call(
        kernel,
        out_shape=(out, out),
        in_specs=[pl.BlockSpec(memory_space=pl.ANY)] * 7,
        out_specs=(pl.BlockSpec(memory_space=pl.ANY),) * 2,
        scratch_shapes=[
            pltpu.VMEM((R, NH * D), BF16),
            pltpu.VMEM((R, NH * D), BF16),
            pltpu.VMEM((R, NH * D), BF16),
            pltpu.VMEM((NH, R), F32),
            pltpu.VMEM((R, D), BF16),
            dma((10,)),
            pltpu.VMEM((NH, R, D), F32),
            dma((NH + 1,)),
            pltpu.VMEM((NZ * R, D), BF16),
            pltpu.VMEM((D + 16, NZ * R), BF16),
            pltpu.VMEM((16, R, D), BF16),
            pltpu.VMEM((16, D + 16, R), F32),
            pltpu.VMEM((16, 8, R), F32),
            pltpu.VMEM((3, NH, D, R), BF16),
            pltpu.VMEM((3, 8, R), F32),
            pltpu.VMEM((3, NH, D, R), BF16),
            pltpu.VMEM((4, 8, R), F32),
            pltpu.VMEM((R, NH * D), F32),
            pltpu.VMEM((R, D), F32),
            pltpu.VMEM((NX, D + 16, D), BF16),
            pltpu.VMEM((NX, D + 16, D), BF16),
            pltpu.VMEM((D + 8, D), F32),
            pltpu.VMEM((D + 8, D), F32),
            pltpu.VMEM((3, D + 8, D), F32),
            pltpu.VMEM((3, D + 8, D), F32),
            pltpu.VMEM((NX, D, D), BF16),
            pltpu.VMEM((NX, D, D), BF16),
            pltpu.VMEM((8, 8, R), F32),
            dma((8,)), dma((8,)), dma((8,)), dma((8,)),
            dma((12,)), dma((12,)), dma((6,)), dma((6,)), dma((4,)), dma((4,)),
            dma((4,)), dma((4,)), dma((3,)), dma((3, 5)), dma((4,)), dma((4,)), dma((8,)), dma((8,)),
        ],
        compiler_params=pltpu.CompilerParams(
            collective_id=0, has_side_effects=True, vmem_limit_bytes=56 << 20
        ),
    )(lin_q, lin_k, lin_v, lin_decay.T, soft_q, soft_k, soft_v)


def solution(mesh):
    spec = P("ctx", "head")
    return jax.shard_map(
        body, mesh=mesh, in_specs=(spec,) * 7, out_specs=(spec, spec), check_vma=False
    )
```

```python
import math

import jax
import jax.numpy as jnp
from jax import lax
from jax.experimental import pallas as pl
from jax.experimental.pallas import tpu as pltpu
from jax.sharding import PartitionSpec as P

MESH = pl.DeviceIdType.MESH
F32 = jnp.float32
BF16 = jnp.bfloat16
D = 128
R = 384
NX = 4
NZ = 8
NH = 4
MODEL = 4096
HIGHEST = lax.Precision.HIGHEST
SCALE = math.log2(math.e) / math.sqrt(D)
START = -1e30
HIDDEN = -2e30

A_BT = (((1,), (1,)), ((), ()))


def dot(a, b):
    return jnp.dot(a, b, preferred_element_type=F32)


def three(a):
    high = a.astype(BF16)
    rest = a - high.astype(F32)
    middle = rest.astype(BF16)
    low = (rest - middle.astype(F32)).astype(BF16)
    at = lax.broadcasted_iota(jnp.int32, (16, D), 0)
    rows = [jnp.broadcast_to(p[0:1].astype(F32), (16, D)) for p in (high, middle, low)]
    out = jnp.where(at == 0, rows[0], jnp.where(at == 1, rows[1], jnp.where(at == 2, rows[2], 0.0)))
    return out.astype(BF16)


def whole(part):
    part = part.astype(F32)
    return part[0:1] + part[1:2] + part[2:3]


def split(a):
    high = a.astype(BF16)
    return high, (a - high.astype(F32)).astype(BF16)


def kernel(
    lq_in, lk_in, lv_in, ld_in, sq, sk_in, sv_in, lin_out, soft_out,
    lq, lk, lv, ld, sv, in_sem, so, out_sem, kb, vb, qb, acc, mx, ob, ls, orv, lrv,
    mixed, cums, p1s, p1r, tot, before, p2s, p2r, p3s, p3r, ssr,
    k_rs, v_rs, k_ss, v_ss, q_rs, q_ss, o_rs, o_ss, l_rs, l_ss,
    p1_rs, p1_ss, p2_rs, p2_ss, p3_rs, p3_ss, s_rs, s_ss,
):
    c = lax.axis_index("ctx")
    hd = lax.axis_index("head")
    z = c // NX
    x = c % NX

    def at_z(dz):
        return (lax.rem(z + dz + NZ, NZ) * NX + x, hd)

    def at_x(dx):
        return (z * NX + lax.rem(x + dx + NX, NX), hd)

    def at_h(dh):
        return (c, lax.rem(hd + dh, 8))

    def rows(r):
        return pl.ds(pl.multiple_of(r * R, R), R)

    def row_of(dz):
        return lax.rem(z + dz + NZ, NZ)

    def remote(src, dst, ss, rs, dev):
        return pltpu.make_async_remote_copy(
            src_ref=src, dst_ref=dst, send_sem=ss, recv_sem=rs, device_id=dev, device_id_type=MESH
        )

    def k_copy(dz, way):
        r = row_of(dz)
        n = 0 if dz == 0 and way > 0 else (1 if dz == 0 else (1 + abs(dz) if way > 0 else 4 + abs(dz)))
        return remote(kb.at[rows(r), :], kb.at[rows(r), :], k_ss.at[n], k_rs.at[r], at_z(way))

    def v_copy(dz, way):
        r = row_of(dz)
        n = 0 if dz == 0 and way > 0 else (1 if dz == 0 else (1 + abs(dz) if way > 0 else 4 + abs(dz)))
        part = vb.at[pl.ds(0, D), rows(r)]
        return remote(part, part, v_ss.at[n], v_rs.at[r], at_z(way))

    k_sends = [(0, 1), (0, -1), (-1, 1), (1, -1), (-2, 1), (2, -1), (-3, 1)]
    v_sends = [(0, 1), (0, -1), (-1, 1), (1, -1), (-2, 1), (2, -1), (3, -1)]

    def tile_of(slot, h):
        return (h, 4 + 2 * ((h + 2) % 4), 5 + 2 * h, 12 + h)[slot]

    def q_copy(slot, h):
        t = tile_of(slot, h)
        if slot < 3:
            src, dx = sq.at[:, pl.ds(h * D, D)], (-1 if slot == 1 else 1)
        elif h < 2:
            src, dx = qb.at[tile_of(2, h)], 1
        else:
            src, dx = qb.at[tile_of(1, h)], -1
        return remote(src, qb.at[t], q_ss.at[t - 4], q_rs.at[t - 4], at_x(dx))

    def o_copy(slot, h):
        dx = (1 if h == 0 else -1) if slot == 3 else (1 if slot == 1 else -1)
        part = pl.ds(h, 2)
        n = 2 * (slot - 1) + h // 2
        return remote(
            ob.at[slot - 1, part], orv.at[slot - 1, part], o_ss.at[n], o_rs.at[n], at_x(dx)
        )

    def l_copy(n):
        dx = (1, -1, 1, -1)[n]
        return remote(ls.at[min(n, 2)], lrv.at[n], l_ss.at[n], l_rs.at[n], at_x(dx))

    def p1_copy(dx):
        there = lax.rem(x + dx, NX)
        return remote(p1s.at[there], p1r.at[x], p1_ss.at[dx], p1_rs.at[x], at_x(dx))

    def p1_wait(dx):
        there = lax.rem(x + dx, NX)
        remote(p1s.at[there], p1r.at[there], p1_ss.at[dx], p1_rs.at[there], at_x(dx)).wait_recv()

    def p2_copy(n, dz):
        return remote(p2s.at[n], p2r.at[n], p2_ss.at[n, dz], p2_rs.at[n], at_z(dz))

    def p2_sends(n):
        return (z % 2 == 0, z % 4 == 1, z == 3)[n]

    def p3_copy(dx):
        there = lax.rem(x + dx, NX)
        return remote(p3s.at[there], p3r.at[x], p3_ss.at[dx], p3_rs.at[x], at_x(dx))

    def p3_wait(dx):
        there = lax.rem(x + dx, NX)
        remote(p3s.at[there], p3r.at[there], p3_ss.at[dx], p3_rs.at[there], at_x(dx)).wait_recv()

    def s_copy(dh):
        return remote(ssr.at[hd], ssr.at[hd], s_ss.at[dh], s_rs.at[hd], at_h(dh))

    def s_wait(dh):
        there = lax.rem(hd + dh, 8)
        remote(ssr.at[there], ssr.at[there], s_ss.at[dh], s_rs.at[there], at_h(dh)).wait_recv()

    places = [(sk_in, kb.at[rows(z), :]), (sv_in, sv), (ld_in, ld), (lk_in, lk), (lv_in, lv), (lq_in, lq)]
    places += [(sq.at[:, pl.ds(h * D, D)], qb.at[h]) for h in range(NH)]
    loads = [pltpu.make_async_copy(a, b, in_sem.at[n]) for n, (a, b) in enumerate(places)]
    for load in loads:
        load.start()
    barrier = pltpu.get_barrier_semaphore()
    for dz in range(1, NZ):
        pl.semaphore_signal(barrier, inc=1, device_id=at_z(dz), device_id_type=MESH)
    for dx in range(1, NX):
        pl.semaphore_signal(barrier, inc=1, device_id=at_x(dx), device_id_type=MESH)
    for dh in range(1, 8):
        pl.semaphore_signal(barrier, inc=1, device_id=at_h(dh), device_id_type=MESH)

    vb[pl.ds(D, 16), :] = jnp.ones((16, NZ * R), BF16)
    loads[1].wait()
    vb[pl.ds(0, D), rows(z)] = sv[...].T
    loads[0].wait()
    pl.semaphore_wait(barrier, 17)

    for way in (1, -1):
        k_copy(0, way).start()
        v_copy(0, way).start()
    q_copy(1, 2).start()
    q_copy(2, 0).start()

    t_at = lax.broadcasted_iota(jnp.int32, (R, R), 0)
    s_at = lax.broadcasted_iota(jnp.int32, (R, R), 1)
    causal = t_at >= s_at
    loads[2].wait()
    decay = jnp.concatenate([ld[...], jnp.zeros((D - NH, R), F32)], axis=0)
    cum_row = lax.dot_general(
        decay, causal.astype(F32), A_BT, precision=HIGHEST, preferred_element_type=F32
    )
    cum = cum_row.T
    cums[...] = cum
    for n in (3, 4):
        loads[n].wait()
    for h in range(NH):
        cols = slice(h * D, (h + 1) * D)
        kh, vh = lk[:, cols], lv[:, cols]
        last = cum[R - 1 : R, h : h + 1]
        high, low = split(kh.astype(F32) * jnp.exp(cum[:, h : h + 1] - last))
        p1s[h, 0:D, :] = (dot(high.T, vh) + dot(low.T, vh)).astype(BF16)
        p1s[h, D : D + 16, :] = three(jnp.broadcast_to(last, (8, D)))
    for dx in range(1, NX):
        p1_copy(dx).start()
    p1r[x] = p1s[x]
    q_copy(1, 3).start()
    q_copy(2, 1).start()
    for h in (0, 1):
        q_copy(1, h).start()
        q_copy(2, h + 2).start()
    loads[5].wait()
    for h in range(NH):
        cols = slice(h * D, (h + 1) * D)
        qh, kh, vh = lq[:, cols], lk[:, cols], lv[:, cols]
        spread = cum[:, h : h + 1] - cum_row[h : h + 1, :]
        scores = lax.dot_general(qh, kh, A_BT, preferred_element_type=F32)
        weights = jnp.where(causal, scores * jnp.exp(-jnp.maximum(spread, 0.0)), 0.0)
        mixed[:, cols] = dot(weights.astype(BF16), vh)

    for_all = jnp.full((8, R), START, F32)
    for t in range(16):
        mx[t] = for_all
        acc[t] = jnp.zeros((D + 16, R), F32)

    diff = s_at - t_at

    def block(i, base, size, masked):
        sub = 768 if size == 768 else 512
        parts = size // sub

        def score(j):
            q = qb[4 * i + j]
            out = []
            for n in range(parts):
                keys = kb[pl.ds(pl.multiple_of(base + n * sub, R if sub == 768 else D), sub), :]
                out.append(lax.dot_general(keys, q, A_BT, preferred_element_type=F32))
            return out

        def finish(j, ps, al):
            total = acc[4 * i + j] * al
            for n in range(parts):
                values = vb[:, pl.ds(pl.multiple_of(base + n * sub, D), sub)]
                total = total + dot(values, ps[n])
            acc[4 * i + j] = total

        now = score(0)
        pending = None
        for j in range(4):
            later = score(j + 1) if j < 3 else None
            if pending is not None:
                finish(*pending)
            if masked:
                dx = jnp.where(i == 0, 0, jnp.where(i == 3, 2, 1 if j % 2 == 0 else -1))
                there = lax.rem(x + dx + NX, NX)
                first = base // R
                halves = []
                for half in range(2):
                    lead = (NX * (z - first - half) + there - x) * R
                    seen = diff + lead >= 0
                    halves.append(jnp.where(seen, now[0][half * R : (half + 1) * R], HIDDEN))
                now = halves
            top = now[0].max(axis=0, keepdims=True)
            for n in range(1, len(now)):
                top = jnp.maximum(top, now[n].max(axis=0, keepdims=True))
            old = mx[4 * i + j, 0:1, :]
            new = jnp.maximum(old, top * SCALE)
            al = jnp.exp2(old - new)
            mx[4 * i + j, 0:1, :] = new
            ps = [jnp.exp2(s * SCALE - new).astype(BF16) for s in now]
            if masked:
                ps = [jnp.concatenate(ps, axis=0)]
            pending = (j, ps, al)
            now = later
        finish(*pending)

    def closed(t):
        l = jnp.maximum(acc[t, D : D + 1, :], 1e-35)
        return acc[t, 0:D, :] / l, mx[t, 0:1, :] + jnp.log2(l)

    def close(slot, heads, part=None):
        for h in heads:
            o, lse = closed(tile_of(slot, h))
            if part is not None:
                other = lrv[part, h : h + 1, :]
                top = jnp.maximum(lse, other)
                w, v = jnp.exp2(lse - top), jnp.exp2(other - top)
                o = (o * w + orv[2, h].astype(F32) * v) / (w + v)
                lse = top + jnp.log2(w + v)
            ob[slot - 1, h] = o.astype(BF16)
            ls[slot - 1, h : h + 1, :] = lse

    def lin_totals():
        for dx in range(1, NX):
            p1_wait(dx)
        total = p1r[0, 0:D, :].astype(F32)
        lead = whole(p1r[0, D : D + 16, :])
        for n in range(1, NX):
            g = whole(p1r[n, D : D + 16, :])
            total = total * jnp.exp(-g) + p1r[n, 0:D, :].astype(F32)
            lead = lead + g
        tot[0:D, :] = total
        tot[D : D + 8, :] = jnp.broadcast_to(lead, (8, D))
        before[...] = jnp.zeros((D + 8, D), F32)
        lin_send(0)

    def lin_send(n):
        @pl.when(p2_sends(n))
        def _():
            g = tot[D : D + 8, :]
            p2s[n, 0:D, :] = before[0:D, :] * jnp.exp(-g[0:1]) + tot[0:D, :]
            p2s[n, D : D + 8, :] = before[D : D + 8, :] + g
            for dz in range(1, 2**n + 1):
                p2_copy(n, dz).start()

    def lin_get(n):
        @pl.when((z % 2 == 1, z % 4 >= 2, z >= 4)[n])
        def _():
            p2_copy(n, 1).wait_recv()
            lead = before[D : D + 8, :]
            before[0:D, :] = p2r[n, 0:D, :] * jnp.exp(-lead[0:1]) + before[0:D, :]
            before[D : D + 8, :] = lead + p2r[n, D : D + 8, :]

    def lin_prefix():
        lin_get(2)
        state = before[0:D, :]
        p3s[0] = state.astype(BF16)
        for n in range(1, NX):
            g = whole(p1r[n - 1, D : D + 16, :])
            state = state * jnp.exp(-g) + p1r[n - 1, 0:D, :].astype(F32)
            p3s[n] = state.astype(BF16)
        for dx in range(1, NX):
            p3_copy(dx).start()
        p3r[x] = p3s[x]

    def lin_mix():
        for dx in range(1, NX):
            p3_wait(dx)
        square = jnp.zeros((R, D), F32)
        for h in range(NH):
            cols = slice(h * D, (h + 1) * D)
            inter = dot(lq[:, cols], p3r[h])
            m = mixed[:, cols] + jnp.exp(-cums[:, h : h + 1]) * inter
            mixed[:, cols] = m
            square = square + m * m
        ssr[hd] = lax.dot_general(
            jnp.ones((8, D), F32), square, A_BT, precision=HIGHEST, preferred_element_type=F32
        )
        for dh in range(1, 8):
            s_copy(dh).start()

    def z_step(d):
        for wait, copy, sends in ((wait_k, k_copy, k_sends), (wait_v, v_copy, v_sends)):
            for dz in (-d, d) if d < 4 else (4,):
                wait(dz)
                for there, way in sends:
                    if there == dz:
                        copy(dz, way).start()

    def wait_k(dz):
        r = row_of(dz)
        part = kb.at[rows(r), :]
        remote(part, part, k_ss.at[0], k_rs.at[r], at_z(1)).wait_recv()

    def wait_v(dz):
        r = row_of(dz)
        part = vb.at[pl.ds(0, D), rows(r)]
        remote(part, part, v_ss.at[0], v_rs.at[r], at_z(1)).wait_recv()

    own = 2 * (z // 2) * R

    def step(n, carry):
        is_a = (n <= 1) | (n == 3) | (n == 5)
        is_b = (n == 2) | (n == 4) | (n == 6) | (n == 10)
        is_c = ((n >= 7) & (n <= 9)) | (n == 11)
        i = jnp.where((n == 0) | (n >= 10), 0, jnp.where((n == 1) | (n == 2) | (n == 8), 1, 3))
        i = jnp.where((n == 3) | (n == 4) | (n == 9), 2, i)

        @pl.when(n == 0)
        def _():
            z_step(1)
            for load in loads[6:]:
                load.wait()

        @pl.when(n == 1)
        def _():
            for h in (0, 1):
                q_copy(2, h).wait_recv()
                q_copy(3, h).start()
                q_copy(1, h + 2).wait_recv()
                q_copy(3, h + 2).start()

        @pl.when(n == 2)
        def _():
            z_step(2)

        @pl.when(n == 3)
        def _():
            for h in (0, 1):
                q_copy(1, h).wait_recv()
                q_copy(2, h + 2).wait_recv()
            lin_totals()

        @pl.when(n == 4)
        def _():
            lin_get(0)
            lin_send(1)

        @pl.when(n == 5)
        def _():
            z_step(3)
            for h in range(NH):
                q_copy(3, h).wait_recv()

        @pl.when(n == 6)
        def _():
            lin_get(1)
            lin_send(2)

        @pl.when(n == 7)
        def _():
            z_step(4)

        @pl.when(n == 8)
        def _():
            lin_prefix()

        @pl.when(n == 11)
        def _():
            lin_mix()

        @pl.when(is_a)
        def _():
            block(i, own, 768, True)

        @pl.when(is_b & ((z == 7) | ((z % 2 == 0) & (z > 0))))
        def _():
            block(i, jnp.where(z == 7, 0, (z - 2) * R), 768, False)

        @pl.when(is_c & (z >= 5))
        def _():
            block(i, jnp.where(z == 7, 2 * R, 0), 1536, False)

        @pl.when(is_c & ((z == 3) | (z == 4)))
        def _():
            block(i, 0 * z, 768, False)

        @pl.when(n == 7)
        def _():
            close(3, range(NH))
            for m in (2, 3):
                l_copy(m).start()
            for h in (0, 2):
                o_copy(3, h).start()

        @pl.when(n == 8)
        def _():
            for slot, h in ((1, 2), (2, 0)):
                close(slot, (h, h + 1))
                o_copy(slot, h).start()

        @pl.when(n == 9)
        def _():
            for m, slot, h in ((2, 1, 0), (3, 2, 2)):
                l_copy(m).wait_recv()
                o_copy(3, h).wait_recv()
                close(slot, (h, h + 1), m)
                l_copy(slot - 1).start()
                o_copy(slot, h).start()

        return carry

    lax.fori_loop(0, 12, step, 0)

    for dh in range(1, 8):
        s_wait(dh)
    square = ssr[0]
    for n in range(1, 8):
        square = square + ssr[n]
    scale = lax.rsqrt(square[0:1, :] * (1.0 / MODEL) + 1e-05)
    scale = jnp.broadcast_to(scale, (D, R)).T
    for h in range(NH):
        cols = slice(h * D, (h + 1) * D)
        mixed[:, cols] = mixed[:, cols] * scale
    stores = [pltpu.make_async_copy(mixed, lin_out, out_sem.at[NH])]
    stores[0].start()

    for m in (0, 1):
        l_copy(m).wait_recv()
    for slot, h in ((1, 2), (2, 0), (1, 0), (2, 2)):
        o_copy(slot, h).wait_recv()
    for h in range(NH):
        o, lse = closed(h)
        others = [lrv[n, h : h + 1, :] for n in range(2)]
        top = jnp.maximum(lse, jnp.maximum(*others))
        w = jnp.exp2(lse - top)
        total = w
        o = o * w
        for n in range(2):
            w = jnp.exp2(others[n] - top)
            total = total + w
            o = o + orv[n, h].astype(F32) * w
        cols = pl.ds(h * D, D)
        so[h] = (o / total).T
        stores.append(pltpu.make_async_copy(so.at[h], soft_out.at[:, cols], out_sem.at[h]))
        stores[-1].start()

    for dz, way in k_sends:
        k_copy(dz, way).wait_send()
    for dz, way in v_sends:
        v_copy(dz, way).wait_send()
    for slot in (1, 2, 3):
        for h in range(NH):
            q_copy(slot, h).wait_send()
        for h in (0, 2):
            o_copy(slot, h).wait_send()
    for m in range(4):
        l_copy(m).wait_send()
    for dx in range(1, NX):
        p1_copy(dx).wait_send()
        p3_copy(dx).wait_send()
    for n in range(3):
        @pl.when(p2_sends(n))
        def _():
            for dz in range(1, 2**n + 1):
                p2_copy(n, dz).wait_send()
    for dh in range(1, 8):
        s_copy(dh).wait_send()

    for store in stores:
        store.wait()

def body(lin_q, lin_k, lin_v, lin_decay, soft_q, soft_k, soft_v):
    dma = pltpu.SemaphoreType.DMA
    out = jax.ShapeDtypeStruct((R, NH * D), F32)
    return pl.pallas_call(
        kernel,
        out_shape=(out, out),
        in_specs=[pl.BlockSpec(memory_space=pl.ANY)] * 7,
        out_specs=(pl.BlockSpec(memory_space=pl.ANY),) * 2,
        scratch_shapes=[
            pltpu.VMEM((R, NH * D), BF16),
            pltpu.VMEM((R, NH * D), BF16),
            pltpu.VMEM((R, NH * D), BF16),
            pltpu.VMEM((NH, R), F32),
            pltpu.VMEM((R, D), BF16),
            dma((10,)),
            pltpu.VMEM((NH, R, D), F32),
            dma((NH + 1,)),
            pltpu.VMEM((NZ * R, D), BF16),
            pltpu.VMEM((D + 16, NZ * R), BF16),
            pltpu.VMEM((16, R, D), BF16),
            pltpu.VMEM((16, D + 16, R), F32),
            pltpu.VMEM((16, 8, R), F32),
            pltpu.VMEM((3, NH, D, R), BF16),
            pltpu.VMEM((3, 8, R), F32),
            pltpu.VMEM((3, NH, D, R), BF16),
            pltpu.VMEM((4, 8, R), F32),
            pltpu.VMEM((R, NH * D), F32),
            pltpu.VMEM((R, D), F32),
            pltpu.VMEM((NX, D + 16, D), BF16),
            pltpu.VMEM((NX, D + 16, D), BF16),
            pltpu.VMEM((D + 8, D), F32),
            pltpu.VMEM((D + 8, D), F32),
            pltpu.VMEM((3, D + 8, D), F32),
            pltpu.VMEM((3, D + 8, D), F32),
            pltpu.VMEM((NX, D, D), BF16),
            pltpu.VMEM((NX, D, D), BF16),
            pltpu.VMEM((8, 8, R), F32),
            dma((8,)), dma((8,)), dma((8,)), dma((8,)),
            dma((12,)), dma((12,)), dma((6,)), dma((6,)), dma((4,)), dma((4,)),
            dma((4,)), dma((4,)), dma((3,)), dma((3, 5)), dma((4,)), dma((4,)), dma((8,)), dma((8,)),
        ],
        compiler_params=pltpu.CompilerParams(
            collective_id=0, has_side_effects=True, vmem_limit_bytes=56 << 20
        ),
    )(lin_q, lin_k, lin_v, lin_decay.T, soft_q, soft_k, soft_v)


def solution(mesh):
    spec = P("ctx", "head")
    return jax.shard_map(
        body, mesh=mesh, in_specs=(spec,) * 7, out_specs=(spec, spec), check_vma=False
    )
```
